512 devices in a mesh: dp: 32 (over x, z), fsdp: 16 (over y, core).
Axes of the slice: x: 4, y: 8, z: 8, core: 2. Of those that a mesh axis runs over, the one named last changes fastest.
Arguments:
- hidden: bfloat16 [32768, 16, 1024], P(('dp', 'fsdp')), may hold values from -108 to 108
- head: bfloat16 [16, 1024, 1024], P('fsdp', 'dp'), may hold values from -14 to 14
- gain: bfloat16 [16, 1024], P('fsdp', 'dp'), may hold values from 0.5 to 1.5
- targets: int32 [32768, 16], P('dp', 'fsdp'), may hold values from 0 to 1023
- lengths: int32 [32], replicated, may hold values from 256 to 1024, as said below
Outputs:
- loss: float32 [], replicated
- grad_hidden: bfloat16 [32768, 16, 1024], P(('dp', 'fsdp'))
- grad_head: float32 [16, 1024, 1024], P('fsdp', 'dp')
The draws below stay inside these ranges and needn't reach their ends.
Inputs may be any that keep to these rules, and one draw needn't show every extreme that they name: `lengths`: each dialogue has at least 256 valid frames, and some dialogue has all 1024.
All inputs are finite; a program needn't handle non-finite values.
Results may differ from the reference program's by a relative error of at most 0.015.
Values may be sent and summed in bfloat16 or wider, within the bound.
A program may use at most 64 MiB of HBM per device.

```python
import math
import jax
import jax.numpy as jnp
from jax import lax

E = 1024
CARD = 1024
LEN = 1024
POS = 16
DIALOGS = 32
FRAMES = 32768


def shared_parts(key):
    row_weights = jnp.exp(jax.random.uniform(jax.random.fold_in(key, 2), (E,), jnp.float32, math.log(0.3), math.log(3.0)))
    return row_weights


def draw_hidden(key, part):
    base = key
    key = jax.random.fold_in(key, 11)
    first, second, third = jax.random.split(key, 3)
    row_weights = shared_parts(base)
    row_scale = jnp.exp(jax.random.uniform(second, (FRAMES, POS, 1), jnp.float32, math.log(0.3), math.log(3.0)))
    col_scale = jnp.exp(jax.random.uniform(third, (1, 1, E), jnp.float32, math.log(0.3), math.log(3.0)))
    frame = jnp.arange(FRAMES, dtype=jnp.int32)
    odd_dialog = frame // LEN % 2 == 1
    emphasis = jnp.where(odd_dialog[:, None, None], row_weights[None, None, :], 1.0)
    values = jax.random.truncated_normal(first, -4.0, 4.0, (FRAMES, POS, E), jnp.float32) * row_scale * col_scale * emphasis
    return values.astype(jnp.bfloat16)


def draw_head(key, part):
    base = key
    key = jax.random.fold_in(key, 23)
    first, second = jax.random.split(key, 2)
    row_weights = shared_parts(base)
    scale = 2.2 / math.sqrt(E)
    col_scale = jnp.exp(jax.random.uniform(second, (1, 1, CARD), jnp.float32, math.log(0.4), math.log(2.5)))
    rows = row_weights[None, :, None]
    values = jax.random.truncated_normal(first, -4.0, 4.0, (POS, E, CARD), jnp.float32) * scale * col_scale * rows
    return values.astype(jnp.bfloat16)


def draw_lengths(key, part):
    key = jax.random.fold_in(key, 37)
    order = jnp.arange(DIALOGS, dtype=jnp.int32)
    rising = LEN // 4 + order * (LEN - LEN // 4) // (DIALOGS - 1)
    jitter = jax.random.randint(key, (DIALOGS,), 0, LEN // 16 + 1)
    values = jnp.maximum(rising - jitter, LEN // 4)
    values = jnp.where(order == 0, LEN // 4, values)
    values = jnp.where(order == DIALOGS - 1, LEN, values)
    return values.astype(jnp.int32)


def plant(values, own_key, smallest, top_value):
    shape = values.shape
    spot = [jax.random.randint(jax.random.fold_in(own_key, axis), (), 0, shape[axis]) for axis in range(len(shape))]
    values = values.at[tuple(spot)].set(smallest)
    longest = shape.index(max(shape))
    spot[longest] = (spot[longest] + 1) % shape[longest]
    return values.at[tuple(spot)].set(top_value)


def setup_inputs(seed: int = 0) -> dict:
    key_of = jax.random.split(jax.random.key(seed), 6)
    hidden = draw_hidden(jax.random.fold_in(key_of[5], 71), 0)
    head = draw_head(jax.random.fold_in(key_of[5], 71), 0)
    gain = jnp.clip(1.0 + 0.1 * jax.random.normal(key_of[2], (POS, E), jnp.float32), 0.5, 1.5).astype(jnp.bfloat16)
    targets = plant(jax.random.randint(key_of[3], (FRAMES, POS), 0, CARD), jax.random.fold_in(key_of[3], 1), 0, CARD - 1).astype(jnp.int32)
    lengths = draw_lengths(jax.random.fold_in(key_of[5], 71), 0)
    return dict(hidden=hidden, head=head, gain=gain, targets=targets, lengths=lengths)


EPS = 1e-05

def reference(hidden, head, gain, targets, lengths):
    frames_all = hidden.reshape(DIALOGS, LEN, POS, E)
    labels_all = targets.reshape(DIALOGS, LEN, POS)
    head_wide = head.astype(jnp.float32)
    gain_wide = gain.astype(jnp.float32)
    classes = jnp.arange(CARD, dtype=jnp.int32)
    slots = jnp.arange(LEN, dtype=jnp.int32)

    def step(carry, inputs):
        grad_sum, loss_sum = carry
        rows, labels, length = inputs
        widened = rows.astype(jnp.float32)
        inverse = lax.rsqrt(lax.optimization_barrier(jnp.mean(widened * widened, axis=-1, keepdims=True)) + EPS)
        normed = (widened * inverse * gain_wide[None, :, :]).astype(jnp.bfloat16)
        normed_wide = lax.optimization_barrier(normed).astype(jnp.float32)
        logits = jnp.einsum('fke,kec->fkc', normed_wide, head_wide)
        top = lax.optimization_barrier(jnp.max(logits, axis=-1, keepdims=True))
        shifted = logits - top
        total = lax.optimization_barrier(jnp.sum(jnp.exp(shifted), axis=-1, keepdims=True))
        log_total = top + jnp.log(total)
        onehot = (labels[:, :, None] == classes[None, None, :]).astype(jnp.float32)
        picked = lax.optimization_barrier(jnp.sum(logits * onehot, axis=-1))
        valid = (slots < length).astype(jnp.float32)
        local = jnp.sum(valid[:, None] * (log_total[:, :, 0] - picked))
        probs = jnp.exp(shifted) / total
        slopes = (valid[:, None, None] * (probs - onehot)).astype(jnp.bfloat16)
        slopes_wide = lax.optimization_barrier(slopes).astype(jnp.float32)
        back = jnp.einsum('fkc,kec->fke', slopes_wide, head_wide)
        weighted = back * gain_wide[None, :, :]
        grad_rows = (inverse * weighted - widened * inverse ** 3 * lax.optimization_barrier(jnp.mean(weighted * widened, axis=-1, keepdims=True))).astype(jnp.bfloat16)
        partial_sum = jnp.einsum('fke,fkc->kec', normed_wide, slopes_wide).astype(jnp.bfloat16)
        partial_sum = lax.optimization_barrier(partial_sum).astype(jnp.float32)
        return ((grad_sum + partial_sum, loss_sum + local), grad_rows)
    init = (jnp.zeros((POS, E, CARD), jnp.float32), jnp.zeros((), jnp.float32))
    (grad_head, loss_sum), grads = lax.scan(step, init, (frames_all, labels_all, lengths))
    loss = loss_sum / (jnp.sum(lengths).astype(jnp.float32) * POS)
    return (loss, grads.reshape(FRAMES, POS, E), grad_head)
```

```python
import jax
import jax.numpy as jnp
from jax import lax
from jax.experimental import pallas as pl
from jax.experimental.pallas import tpu as pltpu
from jax.sharding import PartitionSpec as P

EPS = 1e-05
MESH = pl.DeviceIdType.MESH
NX, NZ, NY, NC = 4, 8, 8, 2
NF = NY * NC
E = 1024
CARD = 1024
CHUNK = 64
ROWS = E // (NX * NZ)
HALF = ROWS // 2
GA, GB = slice(0, 640), slice(640, CARD)
CA = 640
CB = CARD - CA
A, B = slice(0, CA), slice(CA, CARD)

RING_Y = (4, 3, 5, 2, 6, 1, 7)
RING_Z = (4, 3, 5, 2, 6, 1, 7)
RING_X = (2, 1, 3)
RIGHT, LEFT = 0, 1


def mm(a, b, ca, cb):
    return lax.dot_general(
        a, b, (((ca,), (cb,)), ((), ())), preferred_element_type=jnp.float32
    )


def column(row):
    n = row.shape[1]
    r = lax.broadcasted_iota(jnp.int32, (n, n), 0)
    c = lax.broadcasted_iota(jnp.int32, (n, n), 1)
    return jnp.sum(jnp.where(r == c, row, jnp.zeros_like(row)), axis=1, keepdims=True)


def kernel(
    hidden_ref, head_ref, gain_ref, labels_ref, lengths_ref,
    loss_ref, gout_ref, ghead_ref,
    hin, hd, gn, lab, lens, xs, xr, w, nb, sb, gs, dw, xrecv, xsum, zrecv,
    ring, bsum, brecv, sums, xb, xo, lacc, lf, lx, lz,
    hsem, isem, ex_s, ex_r, as_s, as_r,
    waz_s, waz_r, wax_s, wax_r, wbx_s, wbx_r, wbz_s, wbz_r,
    gs_s, gs_r, lsem, rax_s, rax_r, raz_s, raz_r, rbz_s, rbz_r, rbx_s, rbx_r,
    fin_s, fin_r, lfs_s, lfs_r, lxs_s, lxs_r, lzs_s, lzs_r,
):
    dp = lax.axis_index("dp")
    fs = lax.axis_index("fsdp")
    x, z = dp // NZ, lax.rem(dp, NZ)
    y, c = fs // NC, lax.rem(fs, NC)
    h = y // 4
    jme = lax.rem(y, 4) * NC + c

    def ring_y(off):
        return lax.rem(y + off, NY)

    def ring_x(off):
        return lax.rem(x + off, NX)

    def ring_z(off):
        return lax.rem(z + off, NZ)

    def dev_f(yy, cc):
        return (dp, yy * NC + cc)

    def dev_x(off):
        return (ring_x(off) * NZ + z, fs)

    def dev_z(zz):
        return (x * NZ + zz, fs)

    def remote(src, dst, send, recv, device):
        return pltpu.make_async_remote_copy(
            src, dst, send, recv, device_id=device, device_id_type=MESH
        )

    offs_f = [(o, d) for o in RING_Y for d in range(NC)] + [(0, 1)]

    def load(b):
        at = pl.ds(pl.multiple_of(b * 16, 16), 16)
        return pltpu.make_async_copy(hidden_ref.at[at], hin.at[at], hsem.at[b])

    small = [
        pltpu.make_async_copy(head_ref.at[0], hd, isem.at[0]),
        pltpu.make_async_copy(gain_ref, gn, isem.at[1]),
        pltpu.make_async_copy(labels_ref, lab.at[0], isem.at[2]),
        pltpu.make_async_copy(lengths_ref, lens, isem.at[3]),
    ]
    for b in range(4):
        load(b).start()
    for s in small:
        s.start()

    barrier = pltpu.get_barrier_semaphore()
    for o, d in offs_f:
        pl.semaphore_signal(
            barrier, inc=1, device_id=dev_f(ring_y(o), lax.rem(c + d, NC)), device_id_type=MESH
        )
    for o in RING_X:
        pl.semaphore_signal(barrier, inc=1, device_id=dev_x(o), device_id_type=MESH)
    for o in RING_Z:
        pl.semaphore_signal(barrier, inc=1, device_id=dev_z(ring_z(o)), device_id_type=MESH)

    for s in small:
        s.wait()

    gain = column(gn[...].astype(jnp.float32))
    w[0, x, z] = (hd[...].astype(jnp.float32) * gain).astype(jnp.bfloat16)

    r = lax.broadcasted_iota(jnp.int32, (256, 256), 0)
    q = lax.broadcasted_iota(jnp.int32, (256, 256), 1)
    perm = (q == (r & 15) * 16 + (r >> 4)).astype(jnp.bfloat16)

    def split(b, carry):
        at = pl.ds(pl.multiple_of(b * 16, 16), 16)
        load(b).wait()
        block = hin[at].reshape(256, E)
        xs[:, :, at, :] = mm(perm, block, 1, 0).astype(jnp.bfloat16).reshape(2, 8, 16, E)
        return carry

    lax.fori_loop(0, 4, split, 0)

    pl.semaphore_wait(barrier, len(offs_f) + len(RING_X) + len(RING_Z))

    anti = dev_f(ring_y(4), c)
    ex = [
        remote(w.at[0, x, z], w.at[1, x, z], ex_s.at[0], ex_r.at[0], anti),
        remote(lab.at[0], lab.at[1], ex_s.at[1], ex_r.at[1], anti),
    ]
    for e in ex:
        e.start()

    far = 2 + 4 * c
    targets = (
        [(0, 1 - c, c)]
        + [(1, d, 2 + c) for d in range(NC)]
        + [(7, d, 4 + c) for d in range(NC)]
        + [(far, d, 6 + c) for d in range(NC)]
    )

    def a2a(i):
        off, cc, slot = targets[i]
        yy = ring_y(off)
        return remote(
            xs.at[:, lax.rem(yy, 4) * NC + cc], xr.at[:, slot],
            as_s.at[i], as_r.at[slot], dev_f(yy, cc),
        )

    def a2a_in(slot):
        return remote(xr.at[:, slot], xr.at[:, slot], as_s.at[0], as_r.at[slot], dev_f(y, 1 - c))

    def z_way(way):
        return dev_z(ring_z(1 if way == RIGHT else 7))

    def az(role, k, way):
        zz = ring_z(NZ - k) if way == RIGHT else ring_z(k)
        ref = w.at[role, x, zz, :, GA]
        if k == 3:
            ref = w.at[role, x, zz, pl.ds(HALF * way, HALF), GA]
        i = 2 * k + way
        return remote(ref, ref, waz_s.at[role, i], waz_r.at[role, i], z_way(way))

    def ax(role, off, i):
        ref = w.at[role, x, ring_z(off), :, GA]
        n = 3 * off + i
        return remote(ref, ref, wax_s.at[role, n], wax_r.at[role, n], dev_x(RING_X[i]))

    def bx(role, i):
        ref = w.at[role, x, z, :, GB]
        return remote(ref, ref, wbx_s.at[role, i], wbx_r.at[role, i], dev_x(RING_X[i]))

    def bz(role, k, way):
        zz = ring_z(NZ - k) if way == RIGHT else ring_z(k)
        ref = w.at[role, :, zz, :, GB]
        if k == 3:
            ref = w.at[role, pl.ds(2 * way, 2), zz, :, GB]
        i = 2 * k + way
        return remote(ref, ref, wbz_s.at[role, i], wbz_r.at[role, i], z_way(way))

    WAYS = (RIGHT, LEFT)

    def gather(role):
        for way in WAYS:
            az(role, 0, way).start()
        for i in range(3):
            bx(role, i).start()
        for i in range(3):
            ax(role, 0, i).start()

    def az_step(role, k):
        for way in WAYS:
            az(role, k - 1, way).wait_recv()
            if k < 4:
                az(role, k, way).start()
                for i in range(3):
                    ax(role, NZ - k if way == RIGHT else k, i).start()
        if k == 4:
            for i in range(3):
                ax(role, 4, i).start()

    def bz_step(role, k):
        if k == 0:
            for i in range(3):
                bx(role, i).wait_recv()
        for way in WAYS:
            if k > 0:
                bz(role, k - 1, way).wait_recv()
            bz(role, k, way).start()

    def gathered(role):
        for off in range(NZ):
            for i in range(3):
                ax(role, off, i).wait_recv()
        for way in WAYS:
            bz(role, 3, way).wait_recv()

    gather(0)
    for i in (5, 6, 1, 2, 3, 4, 0):
        a2a(i).start()
    xr[:, c] = xs[:, jme]
    az_step(0, 1)
    bz_step(0, 0)
    az_step(0, 2)
    bz_step(0, 1)
    az_step(0, 3)
    ex[0].wait_recv()
    gather(1)
    az_step(0, 4)
    bz_step(0, 2)
    az_step(1, 1)
    bz_step(1, 0)
    az_step(1, 2)
    bz_step(0, 3)
    az_step(1, 3)
    bz_step(1, 1)
    az_step(1, 4)
    ex[1].wait_recv()
    bz_step(1, 2)
    bz_step(1, 3)

    length = lens[dp]
    lacc[...] = jnp.zeros_like(lacc)
    chips = [ring_y(o) for o in (0, 7, 1, 6, 2)]
    lanes = lax.broadcasted_iota(jnp.int32, (1, 128), 1)

    def by_slot(of):
        rows = [of(yy) for yy in chips]
        rows = rows[:3] + [jnp.where(lanes < CHUNK, rows[3], rows[4])]
        return jnp.concatenate([column(row) for row in rows], axis=0)

    frames = by_slot(lambda yy: yy * 128 + lanes)
    valid = (frames < length).astype(jnp.float32)

    sources = [(0, 1 - c, 1 - c)] + [
        (o, d, s) for o, d, s in
        ((7, 0, 2), (7, 1, 3), (1, 0, 4), (1, 1, 5), (6, 0, 6), (2, 1, 7))
    ]

    def half(p):
        return h if p == 0 else 1 - h

    def out(p, i):
        off, cc, slot = sources[i]
        return remote(
            gs.at[p, slot], gout_ref.at[half(p), jme], gs_s.at[p, i], gs_r.at[half(p), jme],
            dev_f(ring_y(off), cc),
        )

    def out_in(p, i):
        j = lax.rem(jme + i, 8)
        return remote(gs.at[p, 0], gout_ref.at[p, j], gs_s.at[p, 0], gs_r.at[p, j], dev_f(y, 1 - c))

    def out_own(p):
        return pltpu.make_async_copy(gs.at[p, c], gout_ref.at[half(p), jme], lsem.at[p])

    def position(p):
        rows = xr[half(p)].reshape(512, E).astype(jnp.float32)
        inverse = lax.rsqrt(jnp.mean(rows * rows, axis=1, keepdims=True) + EPS)
        scaled = rows * inverse
        scaled_b = scaled.astype(jnp.bfloat16)
        nb[...] = scaled_b
        weights = w[p].reshape(E, CARD)
        logits = mm(scaled_b, weights, 1, 0)
        top = jnp.max(logits, axis=1, keepdims=True)
        powers = jnp.exp(logits - top)
        total = jnp.sum(powers, axis=1, keepdims=True)
        labels = by_slot(lambda yy: lab[p, pl.ds(yy, 1), :])
        hit = lax.broadcasted_iota(jnp.int32, (512, CARD), 1) == labels
        picked = jnp.sum(jnp.where(hit, logits, 0.0), axis=1, keepdims=True)
        token = valid * (top + jnp.log(total) - picked)
        lacc[...] += jnp.broadcast_to(jnp.sum(token, axis=0, keepdims=True), (8, 128))
        probs = powers * (valid / total)
        slopes = jnp.where(hit, probs - valid, probs).astype(jnp.bfloat16)
        sb[...] = slopes
        back = mm(slopes, weights, 1, 1)
        mean = jnp.mean(back * scaled, axis=1, keepdims=True)
        gs[p] = (inverse * (back - scaled * mean)).astype(jnp.bfloat16).reshape(8, CHUNK, E)
        for i in (5, 6, 1, 2, 3, 4, 0):
            out(p, i).start()
        out_own(p).start()

    def products(p):
        for xt in range(NX):
            part = mm(nb[:, 256 * xt : 256 * (xt + 1)], sb[...], 0, 0)
            dw[p, xt] = part.astype(jnp.bfloat16).reshape(NZ, ROWS, CARD)

    zg = z // 2

    def group(g):
        return lax.rem(zg + g, 4)

    def rax(role, g, i):
        n = 3 * g + i
        return remote(
            dw.at[role, ring_x(RING_X[i]), pl.ds(2 * group(g), 2), :, A],
            xrecv.at[role, i, pl.ds(2 * g, 2)],
            rax_s.at[role, n], rax_r.at[role, n], dev_x(RING_X[i]),
        )

    def raz(role, g, k):
        return remote(
            xsum.at[role, 2 * g + k], zrecv.at[role, z],
            raz_s.at[role, 2 * g + k], raz_r.at[role, z], dev_z(2 * group(g) + k),
        )

    def raz_own(role):
        k = 1 - lax.rem(z, 2)
        return remote(
            xsum.at[role, k], zrecv.at[role, z], raz_s.at[role, k], raz_r.at[role, z],
            dev_z(2 * zg + k),
        )

    def raz_in(role, i):
        zz = ring_z(i)
        return remote(
            xsum.at[role, 0], zrecv.at[role, zz], raz_s.at[role, 0], raz_r.at[role, zz],
            dev_z(zz),
        )

    def add_x(role, g):
        for i in range(3):
            rax(role, g, i).wait_recv()
        part = dw[role, x, pl.ds(2 * group(g), 2), :, A].astype(jnp.float32)
        for i in range(3):
            part = part + xrecv[role, i, 2 * g : 2 * g + 2].astype(jnp.float32)
        xsum[role, 2 * g : 2 * g + 2] = part.astype(jnp.bfloat16)
        if g:
            for k in range(2):
                raz(role, g, k).start()
        else:
            raz_own(role).start()

    def total_a(role):
        for i in range(1, NZ):
            raz_in(role, i).wait_recv()
        acc = xsum[role, lax.rem(z, 2)].astype(jnp.float32)
        for i in range(1, NZ):
            acc = acc + zrecv[role, ring_z(i)].astype(jnp.float32)
        return acc

    def rbz(role, k, way):
        t = ring_z(4 - k + NZ) if way == RIGHT else ring_z(4 + k)
        half_x = pl.ds(2 * way, 2)
        i = 2 * k + way
        if k == 0:
            src, dst = dw.at[role, half_x, t, :, B], ring.at[role, way, 0, half_x]
        else:
            src, dst = ring.at[role, way, k - 1], ring.at[role, way, k]
        return remote(src, dst, rbz_s.at[role, i], rbz_r.at[role, i], z_way(way))

    def ring_step(role, k):
        for way in WAYS:
            t = ring_z(4 - k + NZ) if way == RIGHT else ring_z(4 + k)
            rbz(role, k - 1, way).wait_recv()
            at = pl.ds(2 * way, 2) if k == 1 else pl.ds(0, 4)
            part = ring[role, way, k - 1, at].astype(jnp.float32)
            part = part + dw[role, at, t, :, B].astype(jnp.float32)
            ring[role, way, k - 1, at] = part.astype(jnp.bfloat16)
            if k == 1:
                at = pl.ds(2 - 2 * way, 2)
                ring[role, way, 0, at] = dw[role, at, t, :, B]
            rbz(role, k, way).start()

    def rbx(role, i):
        return remote(
            bsum.at[role, ring_x(RING_X[i])], brecv.at[role, i],
            rbx_s.at[role, i], rbx_r.at[role, i], dev_x(RING_X[i]),
        )

    def ring_last(role):
        block = dw[role, :, z, :, B].astype(jnp.float32)
        for way in WAYS:
            rbz(role, 3, way).wait_recv()
            block = block + ring[role, way, 3].astype(jnp.float32)
        bsum[role] = block.astype(jnp.bfloat16)
        for i in range(3):
            rbx(role, i).start()

    def total_b(role):
        acc = bsum[role, x].astype(jnp.float32)
        for i in range(3):
            rbx(role, i).wait_recv()
            acc = acc + brecv[role, i].astype(jnp.float32)
        return acc

    def scatter(role):
        for way in WAYS:
            rbz(role, 0, way).start()
        for g in (2, 1, 3, 0):
            for i in range(3):
                rax(role, g, i).start()

    a2a_in(1 - c).wait_recv()
    for slot in range(2, 8):
        a2a_in(slot).wait_recv()
    gathered(1)
    position(1)
    products(1)
    scatter(1)
    gathered(0)
    position(0)
    ring_step(1, 1)
    products(0)
    scatter(0)

    def loss_f(off, d):
        i = off * NC + d
        return remote(
            lf.at[fs], lf.at[fs], lfs_s.at[i], lfs_r.at[i],
            dev_f(ring_y(off), lax.rem(c + d, NC)),
        )

    def loss_x(i):
        return remote(lx.at[x], lx.at[x], lxs_s.at[i], lxs_r.at[i], dev_x(RING_X[i]))

    def loss_z(i):
        return remote(lz.at[z], lz.at[z], lzs_s.at[i], lzs_r.at[i], dev_z(ring_z(RING_Z[i])))

    lf[fs] = lacc[...]
    for o, d in offs_f:
        loss_f(o, d).start()
    add_x(1, 2)
    ring_step(1, 2)
    ring_step(0, 1)
    add_x(1, 1)
    ring_step(1, 3)
    ring_step(0, 2)
    add_x(1, 3)
    for o, d in offs_f:
        loss_f(o, d).wait()
    total_f = lf[0]
    for i in range(1, NF):
        total_f = total_f + lf[i]
    lx[x] = total_f
    for i in range(3):
        loss_x(i).start()
    ring_last(1)
    ring_step(0, 3)
    add_x(1, 0)
    xb[:, B] = total_b(1).astype(jnp.bfloat16)
    add_x(0, 2)
    for i in range(3):
        loss_x(i).wait()
    total_x = lx[0]
    for i in range(1, NX):
        total_x = total_x + lx[i]
    lz[z] = total_x
    for i in range(7):
        loss_z(i).start()
    xb[:, A] = total_a(1).astype(jnp.bfloat16)
    fin = remote(xb, xo, fin_s, fin_r, anti)
    fin.start()
    for e in ex:
        e.wait_send()
    for i in range(7):
        a2a(i).wait_send()
    for role in range(2):
        for k in range(4):
            for way in WAYS:
                az(role, k, way).wait_send()
                bz(role, k, way).wait_send()
        for i in range(3):
            bx(role, i).wait_send()
            for off in range(NZ):
                ax(role, off, i).wait_send()

    add_x(0, 1)
    ring_last(0)
    add_x(0, 3)
    add_x(0, 0)
    sums[:, B] = total_b(0)
    sums[:, A] = total_a(0)
    for i in range(7):
        loss_z(i).wait()
    total_z = lz[0]
    for i in range(1, NZ):
        total_z = total_z + lz[i]
    tokens = lens[0]
    for i in range(1, NX * NZ):
        tokens = tokens + lens[i]
    count = jnp.full((8, 128), tokens, jnp.int32).astype(jnp.float32) * NF
    loss_ref[...] = (total_z / count)[0:1, 0:1]

    fin.wait()
    ghead_ref[0] = (sums[...] + xo[...].astype(jnp.float32)) * gain

    for role in range(2):
        for k in range(4):
            for way in WAYS:
                rbz(role, k, way).wait_send()
        for i in range(3):
            rbx(role, i).wait_send()
            for g in range(4):
                rax(role, g, i).wait_send()
        for g in range(1, 4):
            for k in range(2):
                raz(role, g, k).wait_send()
        raz_own(role).wait_send()
    for p in range(2):
        for i in range(7):
            out(p, i).wait_send()
        for i in range(1, 8):
            out_in(p, i).wait_recv()
        out_own(p).wait()


def per_device(hidden, head, gain, targets, lengths):
    labels = targets.reshape(NY, 128)
    vmem = pl.BlockSpec(memory_space=pltpu.VMEM)
    hbm = pl.BlockSpec(memory_space=pltpu.HBM)
    bf = lambda *s: pltpu.VMEM(s, jnp.bfloat16)
    f32 = lambda *s: pltpu.VMEM(s, jnp.float32)
    dma = lambda *s: pltpu.SemaphoreType.DMA(s)
    one = pltpu.SemaphoreType.DMA
    pair = lambda *s: [dma(*s), dma(*s)]
    loss, grad, grad_head = pl.pallas_call(
        kernel,
        out_shape=(
            jax.ShapeDtypeStruct((1, 1), jnp.float32),
            jax.ShapeDtypeStruct((2, 8, CHUNK, E), jnp.bfloat16),
            jax.ShapeDtypeStruct((1, ROWS, CARD), jnp.float32),
        ),
        in_specs=[hbm] * 5,
        out_specs=(vmem, pl.BlockSpec(memory_space=pl.ANY), vmem),
        scratch_shapes=[
            bf(CHUNK, NF, E), bf(ROWS, CARD), bf(1, ROWS),
            pltpu.VMEM((2, NY, 128), jnp.int32), pltpu.SMEM((NX * NZ,), jnp.int32),
            bf(2, 8, CHUNK, E), bf(2, 8, CHUNK, E), bf(2, NX, NZ, ROWS, CARD),
            bf(512, E), bf(512, CARD), bf(2, 8, CHUNK, E), bf(2, NX, NZ, ROWS, CARD),
            bf(2, 3, NZ, ROWS, CA), bf(2, NZ, ROWS, CA), bf(2, NZ, ROWS, CA),
            bf(2, 2, 4, NX, ROWS, CB), bf(2, NX, ROWS, CB), bf(2, 3, ROWS, CB),
            f32(ROWS, CARD), bf(ROWS, CARD), bf(ROWS, CARD),
            f32(8, 128), f32(NF, 8, 128), f32(NX, 8, 128), f32(NZ, 8, 128),
            dma(4), dma(4), *pair(2), dma(7), dma(8),
            *pair(2, 8), *pair(2, 24), *pair(2, 3), *pair(2, 8),
            dma(2, 7), dma(2, 8), dma(2), *pair(2, 12), *pair(2, 8), *pair(2, 8), *pair(2, 3),
            one, one, *pair(16), *pair(3), *pair(7),
        ],
        compiler_params=pltpu.CompilerParams(
            collective_id=0, has_side_effects=True, vmem_limit_bytes=46 << 20
        ),
        cost_estimate=pl.CostEstimate(
            flops=6 * 1024**3, bytes_accessed=4 << 20, transcendentals=1 << 20
        ),
    )(*(pltpu.with_memory_space_constraint(a, pltpu.HBM) for a in (hidden, head, gain, labels, lengths)))
    grad = jnp.transpose(grad.reshape(NF, CHUNK, E), (1, 0, 2))
    return loss[0, 0], grad, grad_head


def solution(mesh):
    placed = (
        P(("dp", "fsdp"), None, None),
        P("fsdp", "dp", None),
        P("fsdp", "dp"),
        P("dp", "fsdp"),
        P(),
    )
    return jax.shard_map(
        per_device,
        mesh=mesh,
        in_specs=placed,
        out_specs=(P(), P(("dp", "fsdp"), None, None), P("fsdp", "dp", None)),
        check_vma=False,
    )
```
